512 devices in a mesh: owner: 64 (over y, z), grp: 8 (over x, core).
Axes of the slice: x: 4, y: 4, z: 16, core: 2. Of those that a mesh axis runs over, the one named last changes fastest.
Arguments:
- sources: bfloat16 [16, 524288], P(None, ('owner', 'grp')), may hold values from -6 to 6
- near_pairs: int32 [8192, 2], P(('owner', 'grp')), may hold values from 0 to 2047, as said below
- near_blocks: bfloat16 [8192, 256, 256], P(('owner', 'grp')), may hold values from -0.375 to 0.375
- far_pairs: int32 [32768, 2], P(('owner', 'grp')), may hold values from 0 to 2047, as said below
- far_left: bfloat16 [32768, 32, 256], P(('owner', 'grp')), may hold values from -1 to 1
- far_right: bfloat16 [32768, 32, 256], P(('owner', 'grp')), may hold values from -0.375 to 0.375
Outputs:
- potential: bfloat16 [16, 524288], P(None, ('owner', 'grp'))
The draws below stay inside these ranges and needn't reach their ends.
Inputs may be any that keep to these rules, and one draw needn't show every extreme that they name: `near_pairs`: each row is (target, source); the target is a cluster held by the device that holds the row, and the source a cluster held by a device with the same owner index. `far_pairs`: each row is (target, source); the target is a cluster held by the device that holds the row, and the source a cluster held by a device with the same grp index. The rows of one device name sources on one owner index at most 2 times, and exactly 2 times for some owner index.
All inputs are finite; a program needn't handle non-finite values.
Results may differ from the reference program's by a relative error of at most 0.0085.
Values may be sent and summed in bfloat16 or wider, within the bound.
No kernel may reach another device: no remote copies, remote signals or barrier semaphores. Data moves between devices by JAX's collectives and lax.ppermute only.
A program may use at most 64 MiB of HBM per device.

```python
import jax
import jax.numpy as jnp
from jax import lax

P_SIZE = 256
K = 32
R = 16
CAP = 2
CL = 4
NEAR_DEV = 16
FAR_DEV = 64
NCL = 2048
NPAN = 524288
NNEAR = 8192
NFAR = 32768
N_OWNER = 64
N_GRP = 8
DEVICES = 512


def draw_near_pairs(key, part):
    key = jax.random.fold_in(key, 5)

    def one_device(device):
        sub = jax.random.fold_in(key, device)
        first, second, third = jax.random.split(sub, 3)
        region = device // N_GRP
        target = device * CL + jax.random.randint(first, (NEAR_DEV,), 0, CL)
        holder = region * N_GRP + jax.random.randint(second, (NEAR_DEV,), 0, N_GRP)
        source = holder * CL + jax.random.randint(third, (NEAR_DEV,), 0, CL)
        return jnp.stack([target, source], axis=1)
    rows = jax.vmap(one_device)(jnp.arange(DEVICES))
    return rows.reshape(DEVICES * NEAR_DEV, 2).astype(jnp.int32)


def draw_far_pairs(key, part):
    key = jax.random.fold_in(key, 11)

    def one_device(device):
        sub = jax.random.fold_in(key, device)
        first, second, third, fourth = jax.random.split(sub, 4)
        count = N_OWNER * CAP
        slots = jnp.arange(count)
        ranking = jax.random.permutation(first, count)
        filled = jax.random.randint(second, (), 0, N_OWNER)
        scores = jnp.where(slots // CAP == filled, ranking - count, ranking)
        chosen = jnp.argsort(scores, stable=True)[:FAR_DEV]
        peers = chosen // CAP
        holder = peers * N_GRP + device % N_GRP
        source = holder * CL + jax.random.randint(third, (FAR_DEV,), 0, CL)
        target = device * CL + jax.random.randint(fourth, (FAR_DEV,), 0, CL)
        return jnp.stack([target, source], axis=1)
    rows = jax.vmap(one_device)(jnp.arange(DEVICES))
    return rows.reshape(DEVICES * FAR_DEV, 2).astype(jnp.int32)


def levels(stream_key, extent, cuts, least, top_value):
    def one(axis_at, shards_of):
        draws = jax.random.uniform(jax.random.fold_in(jax.random.fold_in(stream_key, 6), axis_at), (shards_of,), jnp.float32, least / len(cuts), top_value / len(cuts))
        return jnp.repeat(jnp.exp(draws), extent[axis_at] // shards_of).reshape((-1,) + (1,) * (len(extent) - axis_at - 1))

    gain = one(*cuts[0])
    for cut in cuts[1:]:
        gain = gain * one(*cut)
    return gain


def scatter_about(key, dims, deviation, bound, cuts=(), dtype=jnp.bfloat16):
    loudness = levels(key, dims, cuts, -0.22, 0.18) if cuts else 1.0
    values = jax.random.normal(key, dims, jnp.float32) * deviation * loudness
    return jnp.minimum(jnp.maximum(values, -bound), bound).astype(dtype)


def setup_inputs(seed: int = 0) -> dict:
    splits = jax.random.split(jax.random.key(seed), 7)
    return {
        "sources": scatter_about(splits[0], (R, NPAN), 1.0, 6.0, ((1, 512),)),
        "near_pairs": draw_near_pairs(jax.random.fold_in(splits[6], 71), 0),
        "near_blocks": scatter_about(splits[2], (NNEAR, P_SIZE, P_SIZE), P_SIZE ** -0.5, 0.375, ((0, 512),)),
        "far_pairs": draw_far_pairs(jax.random.fold_in(splits[6], 71), 0),
        "far_left": scatter_about(splits[4], (NFAR, K, P_SIZE), K ** -0.5, 1.0, ((0, 512),)),
        "far_right": scatter_about(splits[5], (NFAR, K, P_SIZE), P_SIZE ** -0.5, 0.375, ((0, 512),)),
    }


def reference(sources, near_pairs, near_blocks, far_pairs, far_left, far_right):
    whole = sources.astype(jnp.float32).reshape(R, NCL, P_SIZE)
    total = jnp.zeros((R, NCL, P_SIZE), jnp.float32)

    def near_step(total, item):
        pairs, blocks = item
        target = pairs[:, 0].astype(jnp.int32)
        source = pairs[:, 1].astype(jnp.int32)
        blocks = blocks.astype(jnp.float32)
        forward = jnp.einsum("rnq,npq->rnp", whole[:, source], blocks)
        backward = jnp.einsum("rnp,npq->rnq", whole[:, target], blocks)
        total = total.at[:, target].add(forward)
        total = total.at[:, source].add(backward)
        return total, None

    total, _ = lax.scan(near_step, total, (near_pairs.reshape(DEVICES, NEAR_DEV, 2), near_blocks.reshape(DEVICES, NEAR_DEV, P_SIZE, P_SIZE)))

    def far_step(total, item):
        pairs, left, right = item
        target = pairs[:, 0].astype(jnp.int32)
        source = pairs[:, 1].astype(jnp.int32)
        left = left.astype(jnp.float32)
        right = right.astype(jnp.float32)
        coef = jnp.einsum("rnq,nkq->rnk", whole[:, source], right).astype(jnp.bfloat16).astype(jnp.float32)
        total = total.at[:, target].add(jnp.einsum("rnk,nkp->rnp", coef, left))
        coef_back = jnp.einsum("rnp,nkp->rnk", whole[:, target], left).astype(jnp.bfloat16).astype(jnp.float32)
        total = total.at[:, source].add(jnp.einsum("rnk,nkq->rnq", coef_back, right))
        return total, None

    total, _ = lax.scan(far_step, total, (far_pairs.reshape(DEVICES, FAR_DEV, 2), far_left.reshape(DEVICES, FAR_DEV, K, P_SIZE), far_right.reshape(DEVICES, FAR_DEV, K, P_SIZE)))
    return total.reshape(R, NPAN).astype(jnp.bfloat16)
```

```python
import jax
import jax.numpy as jnp
from jax import lax
from jax.experimental import pallas as pl
from jax.experimental.pallas import tpu as pltpu
from jax.sharding import Mesh
from jax.sharding import PartitionSpec as P

RHS = 16
PANELS = 256
RANK = 32
CAP = 2
CL = 4
NY = 4
NZH = 8
NZL = 2
NX = 4
NC = 2
GRP = NX * NC
PEERS = NY * NZL
SLOTS = NZH * CAP
NEAR = 16
FAR = 64
BATCH = 8
GROUPS = FAR // BATCH
ROWS = BATCH * RHS
F32 = jnp.float32
BF16 = jnp.bfloat16

VMEM = pl.BlockSpec(memory_space=pltpu.VMEM)
SMEM = pl.BlockSpec(memory_space=pltpu.SMEM)
ANY = pl.BlockSpec(memory_space=pl.ANY)
WHOLE = pl.BlockSpec()


def call(kernel, out_shape, in_specs, out_specs, scratch=(), cost=(0, 0)):
    return pl.pallas_call(
        kernel,
        out_shape=out_shape,
        in_specs=in_specs,
        out_specs=out_specs,
        scratch_shapes=list(scratch),
        compiler_params=pltpu.CompilerParams(vmem_limit_bytes=24 * 1024 * 1024),
        cost_estimate=pl.CostEstimate(flops=cost[0], bytes_accessed=cost[1], transcendentals=0),
    )


def dot_nt(a, b):
    return lax.dot_general(a, b, (((1,), (1,)), ((), ())), preferred_element_type=F32)


def dot_nn(a, b):
    return lax.dot_general(a, b, (((1,), (0,)), ((), ())), preferred_element_type=F32)


def diagonal_mask():
    row = lax.broadcasted_iota(jnp.int32, (ROWS, PANELS), 0) // RHS
    col = lax.broadcasted_iota(jnp.int32, (ROWS, PANELS), 1) // RANK
    return row == col


def spread_kernel(x_ref, out_ref, local_ref):
    for c in range(CL):
        block = x_ref[:, c * PANELS:(c + 1) * PANELS]
        local_ref[c] = block
        for d in range(out_ref.shape[0]):
            out_ref[d, c] = block


def backward_kernel(
    near_ref, far_ref, x_ref, blocks_hbm, left_hbm, right_hbm,
    near_hbm, far_hbm, slot_out,
    count, table, near_sum, blocks_ref, left_ref, right_ref, near_out, far_out, sems,
):
    loads = [
        pltpu.make_async_copy(left_hbm, left_ref, sems.at[0]),
        pltpu.make_async_copy(right_hbm, right_ref, sems.at[1]),
        pltpu.make_async_copy(blocks_hbm, blocks_ref, sems.at[2]),
    ]
    for load in loads:
        load.start()

    def clear(o, _):
        count[o] = 0
        return 0

    lax.fori_loop(0, NY * NZH * NZL, clear, 0)
    table[...] = jnp.zeros(table.shape, F32)
    far_out[...] = jnp.zeros(far_out.shape, BF16)

    def place(n, _):
        source = far_ref[1, n]
        owner = source // (GRP * CL)
        order = count[owner]
        count[owner] = order + 1
        y = owner // (NZH * NZL)
        zh = (owner // NZL) % NZH
        zl = owner % NZL
        peer = y * NZL + zl
        within = zh * CAP + order
        slot_out[n] = peer * (SLOTS + 1) + within
        table[pl.ds(peer * SLOTS + within, 1), :] = jnp.full((1, PANELS), (source % CL).astype(F32))
        return 0

    lax.fori_loop(0, FAR, place, 0)
    for m in range(PEERS):
        far_out[m * (SLOTS + 1) + SLOTS] = table[m * SLOTS:(m + 1) * SLOTS, :].astype(BF16)
    loads[0].wait()
    loads[1].wait()
    mask = diagonal_mask()
    for g in range(GROUPS):
        xt = jnp.concatenate(
            [x_ref[far_ref[0, g * BATCH + i] % CL] for i in range(BATCH)], axis=0
        )
        left = left_ref[g * BATCH:(g + 1) * BATCH].reshape(BATCH * RANK, PANELS)
        right = right_ref[g * BATCH:(g + 1) * BATCH].reshape(BATCH * RANK, PANELS)
        coef = jnp.where(mask, dot_nt(xt, left), 0.0).astype(BF16)
        term = dot_nn(coef, right).astype(BF16)
        for i in range(BATCH):
            far_out[slot_out[g * BATCH + i]] = term[i * RHS:(i + 1) * RHS, :]
    far_store = pltpu.make_async_copy(far_out, far_hbm, sems.at[3])
    far_store.start()
    near_sum[...] = jnp.zeros(near_sum.shape, F32)
    loads[2].wait()
    for n in range(NEAR):
        source = near_ref[1, n] % (GRP * CL)
        near_sum[source] += dot_nn(x_ref[near_ref[0, n] % CL], blocks_ref[n])
    for d in range(GRP):
        near_out[d, 0] = x_ref[...]
        near_out[d, 1] = near_sum[d * CL:(d + 1) * CL].astype(BF16)
    near_store = pltpu.make_async_copy(near_out, near_hbm, sems.at[4])
    near_store.start()
    far_store.wait()
    near_store.wait()


def pick_kernel(x_ref, table_ref, out_ref):
    def peer(m, _):
        table = table_ref[m, SLOTS].astype(F32)
        for s in range(SLOTS):
            want = jnp.broadcast_to(table[s:s + 1, :], (RHS, PANELS))
            block = x_ref[s // CAP, 0].astype(F32)
            for c in range(1, CL):
                block = jnp.where(want == c, x_ref[s // CAP, c].astype(F32), block)
            out_ref[m, s] = block.astype(BF16)
        return 0

    lax.fori_loop(0, PEERS, peer, 0)


def merge_kernel(in_ref, out_ref):
    tables = [in_ref[m, SLOTS].astype(F32) for m in range(PEERS)]
    for zh in range(NZH):
        sums = [jnp.zeros((RHS, PANELS), F32) for _ in range(CL)]
        for m in range(PEERS):
            for s in range(zh * CAP, (zh + 1) * CAP):
                block = in_ref[m, s].astype(F32)
                want = jnp.broadcast_to(tables[m][s:s + 1, :], (RHS, PANELS))
                for c in range(CL):
                    sums[c] = sums[c] + jnp.where(want == c, block, 0.0)
        for c in range(CL):
            out_ref[zh, c] = sums[c].astype(BF16)


def near_kernel(near_ref, got_ref, blocks_ref, out_ref):
    for c in range(CL):
        total = got_ref[0, 1, c].astype(F32)
        for d in range(1, GRP):
            total = total + got_ref[d, 1, c].astype(F32)
        out_ref[c] = total
    for n in range(NEAR):
        source = near_ref[1, n] % (GRP * CL)
        block = got_ref[source // CL, 0, source % CL]
        out_ref[near_ref[0, n] % CL] += dot_nt(block, blocks_ref[n])


def far_kernel(far_ref, slot_ref, x_ref, left_ref, right_ref, out_ref, spread):
    mask = diagonal_mask()
    total = jnp.zeros((CL * RHS, PANELS), F32)
    spread[...] = jnp.zeros(spread.shape, F32)
    for g in range(GROUPS):
        slots = [slot_ref[g * BATCH + i] for i in range(BATCH)]
        xs = jnp.concatenate([x_ref[s - s // (SLOTS + 1)] for s in slots], axis=0)
        left = left_ref[g * BATCH:(g + 1) * BATCH].reshape(BATCH * RANK, PANELS)
        right = right_ref[g * BATCH:(g + 1) * BATCH].reshape(BATCH * RANK, PANELS)
        coef = jnp.where(mask, dot_nt(xs, right), 0.0)
        for i in range(BATCH):
            target = far_ref[0, g * BATCH + i] % CL
            spread[g, target] += coef[i * RHS:(i + 1) * RHS, :]
        total = total + dot_nn(spread[g].reshape(CL * RHS, PANELS).astype(BF16), left)
    out_ref[...] = total.reshape(CL, RHS, PANELS)


def final_kernel(near_ref, far_ref, far_in, out_ref):
    for c in range(CL):
        total = near_ref[c] + far_ref[c]
        for z in range(NZH):
            total = total + far_in[z, c].astype(F32)
        out_ref[:, c * PANELS:(c + 1) * PANELS] = total.astype(BF16)


def shape(dims, dtype=BF16):
    return jax.ShapeDtypeStruct(dims, dtype)


def on_device(sources, near_pairs, near_blocks, far_pairs, far_left, far_right):
    near_table = near_pairs.T
    far_table = far_pairs.T
    spread, local = call(
        spread_kernel,
        (shape((NZH, CL, RHS, PANELS)), shape((CL, RHS, PANELS))),
        [VMEM],
        (WHOLE, VMEM),
        cost=(0, 300000),
    )(sources)
    along_z = lax.all_to_all(spread, "zh", 0, 0, tiled=True)
    near_send, far_send, slots = call(
        backward_kernel,
        (
            shape((GRP, 2, CL, RHS, PANELS)),
            shape((PEERS * (SLOTS + 1), RHS, PANELS)),
            shape((FAR,), jnp.int32),
        ),
        [SMEM, SMEM, VMEM, ANY, ANY, ANY],
        (ANY, ANY, SMEM),
        [
            pltpu.SMEM((NY * NZH * NZL,), jnp.int32),
            pltpu.VMEM((PEERS * SLOTS, PANELS), F32),
            pltpu.VMEM((GRP * CL, RHS, PANELS), F32),
            pltpu.VMEM(near_blocks.shape, BF16),
            pltpu.VMEM(far_left.shape, BF16),
            pltpu.VMEM(far_right.shape, BF16),
            pltpu.VMEM((GRP, 2, CL, RHS, PANELS), BF16),
            pltpu.VMEM((PEERS * (SLOTS + 1), RHS, PANELS), BF16),
            pltpu.SemaphoreType.DMA((5,)),
        ],
        cost=(2000000000, 6000000),
    )(near_table, far_table, local, near_blocks, far_left, far_right)
    region = lax.all_to_all(near_send, ("x", "c"), 0, 0, tiled=True)
    far_got = lax.all_to_all(
        far_send.reshape(PEERS, SLOTS + 1, RHS, PANELS), ("y", "zl"), 0, 0, tiled=True
    )
    picked = call(
        pick_kernel,
        shape((PEERS, SLOTS, RHS, PANELS)),
        [VMEM, VMEM],
        WHOLE,
        cost=(0, 2000000),
    )(along_z, far_got)
    far_sources = lax.all_to_all(picked, ("y", "zl"), 0, 0, tiled=True)
    merged = call(
        merge_kernel, shape((NZH, CL, RHS, PANELS)), [VMEM], WHOLE, cost=(0, 2000000)
    )(far_got)
    far_back = lax.all_to_all(merged, "zh", 0, 0, tiled=True)
    near_total = call(
        near_kernel,
        shape((CL, RHS, PANELS), F32),
        [SMEM, VMEM, VMEM],
        VMEM,
        cost=(500000000, 2500000),
    )(near_table, region, near_blocks)
    far_total = call(
        far_kernel,
        shape((CL, RHS, PANELS), F32),
        [SMEM, SMEM, VMEM, VMEM, VMEM],
        VMEM,
        [pltpu.VMEM((GROUPS, CL, RHS, PANELS), F32)],
        cost=(1000000000, 3500000),
    )(far_table, slots, far_sources.reshape(PEERS * SLOTS, RHS, PANELS), far_left, far_right)
    return call(
        final_kernel, shape(sources.shape), [VMEM] * 3, VMEM, cost=(0, 1000000)
    )(near_total, far_total, far_back)


def solution(mesh):
    axes = ("y", "zh", "zl", "x", "c")
    fine = Mesh(mesh.devices.reshape(NY, NZH, NZL, NX, NC), axes)
    placed = (
        P(None, axes),
        P(axes, None),
        P(axes, None, None),
        P(axes, None),
        P(axes, None, None),
        P(axes, None, None),
    )
    return jax.shard_map(
        on_device, mesh=fine, in_specs=placed, out_specs=P(None, axes), check_vma=False
    )
```

```python
import jax
import jax.numpy as jnp
from jax import lax
from jax.experimental import pallas as pl
from jax.experimental.pallas import tpu as pltpu
from jax.sharding import Mesh
from jax.sharding import PartitionSpec as P

RHS = 16
PANELS = 256
RANK = 32
CAP = 2
CL = 4
NY = 4
NZH = 8
NZL = 2
NX = 4
NC = 2
GRP = NX * NC
PEERS = NY * NZL
SLOTS = NZH * CAP
NEAR = 16
FAR = 64
BATCH = 8
GROUPS = FAR // BATCH
ROWS = BATCH * RHS
F32 = jnp.float32
BF16 = jnp.bfloat16

VMEM = pl.BlockSpec(memory_space=pltpu.VMEM)
SMEM = pl.BlockSpec(memory_space=pltpu.SMEM)
ANY = pl.BlockSpec(memory_space=pl.ANY)
WHOLE = pl.BlockSpec()


def call(kernel, out_shape, in_specs, out_specs, scratch=(), cost=(0, 0), vmem=24):
    return pl.pallas_call(
        kernel,
        out_shape=out_shape,
        in_specs=in_specs,
        out_specs=out_specs,
        scratch_shapes=list(scratch),
        compiler_params=pltpu.CompilerParams(vmem_limit_bytes=vmem * 1024 * 1024),
        cost_estimate=pl.CostEstimate(flops=cost[0], bytes_accessed=cost[1], transcendentals=0),
    )


def dot_nt(a, b):
    return lax.dot_general(a, b, (((1,), (1,)), ((), ())), preferred_element_type=F32)


def dot_nn(a, b):
    return lax.dot_general(a, b, (((1,), (0,)), ((), ())), preferred_element_type=F32)


def diagonal_mask():
    row = lax.broadcasted_iota(jnp.int32, (ROWS, PANELS), 0) // RHS
    col = lax.broadcasted_iota(jnp.int32, (ROWS, PANELS), 1) // RANK
    return row == col


def far_send_kernel(
    far_ref, x_hbm, left_hbm, right_hbm, out_hbm, slot_out,
    count, table, x_ref, left_ref, right_ref, out_ref, sems,
):
    loads = [
        pltpu.make_async_copy(x_hbm, x_ref, sems.at[0]),
        pltpu.make_async_copy(left_hbm, left_ref, sems.at[1]),
        pltpu.make_async_copy(right_hbm, right_ref, sems.at[2]),
    ]
    for load in loads:
        load.start()

    def clear(o, _):
        count[o] = 0
        return 0

    lax.fori_loop(0, NY * NZH * NZL, clear, 0)
    table[...] = jnp.zeros(table.shape, F32)
    out_ref[...] = jnp.zeros(out_ref.shape, BF16)

    def place(n, _):
        source = far_ref[1, n]
        owner = source // (GRP * CL)
        order = count[owner]
        count[owner] = order + 1
        y = owner // (NZH * NZL)
        zh = (owner // NZL) % NZH
        zl = owner % NZL
        peer = y * NZL + zl
        within = zh * CAP + order
        slot_out[n] = peer * (SLOTS + 1) + within
        table[pl.ds(peer * SLOTS + within, 1), :] = jnp.full((1, PANELS), (source % CL).astype(F32))
        return 0

    lax.fori_loop(0, FAR, place, 0)
    for m in range(PEERS):
        out_ref[m * (SLOTS + 1) + SLOTS] = table[m * SLOTS:(m + 1) * SLOTS, :].astype(BF16)
    for load in loads:
        load.wait()
    mask = diagonal_mask()
    for g in range(GROUPS):
        targets = [far_ref[0, g * BATCH + i] % CL for i in range(BATCH)]
        xt = jnp.concatenate(
            [x_ref[:, pl.ds(pl.multiple_of(t * PANELS, PANELS), PANELS)] for t in targets], axis=0
        )
        left = left_ref[g * BATCH:(g + 1) * BATCH].reshape(BATCH * RANK, PANELS)
        right = right_ref[g * BATCH:(g + 1) * BATCH].reshape(BATCH * RANK, PANELS)
        coef = jnp.where(mask, dot_nt(xt, left), 0.0).astype(BF16)
        term = dot_nn(coef, right).astype(BF16)
        for i in range(BATCH):
            out_ref[slot_out[g * BATCH + i]] = term[i * RHS:(i + 1) * RHS, :]
    store = pltpu.make_async_copy(out_ref, out_hbm, sems.at[3])
    store.start()
    store.wait()


def near_send_kernel(near_ref, x_ref, blocks_ref, swap_out, own_out, near_sum):
    x = lax.axis_index("x")
    c = lax.axis_index("c")
    for w in range(CL):
        swap_out[0, w] = x_ref[:, w * PANELS:(w + 1) * PANELS]
    near_sum[...] = jnp.zeros(near_sum.shape, F32)
    for n in range(NEAR):
        source = near_ref[1, n] % (GRP * CL)
        start = pl.multiple_of((near_ref[0, n] % CL) * PANELS, PANELS)
        near_sum[source] += dot_nn(x_ref[:, pl.ds(start, PANELS)], blocks_ref[n])
    for k in range(NX):
        at = ((x + k) % NX) * (NC * CL)
        own_out[k] = near_sum[pl.ds(at + c * CL, CL)]
        swap_out[1 + k] = near_sum[pl.ds(at + (1 - c) * CL, CL)].astype(BF16)


def near_pack_kernel(x_ref, own_ref, got_ref, home_ref, *out_refs):
    home_ref[...] = own_ref[0] + got_ref[1].astype(F32)
    for k in range(1, NX):
        out = out_refs[k - 1]
        for w in range(CL):
            out[0, w] = x_ref[:, w * PANELS:(w + 1) * PANELS]
        out[1] = got_ref[0]
        out[2] = (own_ref[k] + got_ref[1 + k].astype(F32)).astype(BF16)


def pick_kernel(x_ref, table_ref, after_ref, out_ref):
    def peer(m, _):
        table = table_ref[m, SLOTS].astype(F32)
        for s in range(SLOTS):
            want = jnp.broadcast_to(table[s:s + 1, :], (RHS, PANELS))
            block = x_ref[s // CAP, 0, 0].astype(F32)
            for w in range(1, CL):
                block = jnp.where(want == w, x_ref[s // CAP, 0, w].astype(F32), block)
            out_ref[m, s] = block.astype(BF16)
        return 0

    lax.fori_loop(0, PEERS, peer, 0)


def merge_kernel(x_ref, in_ref, out_ref):
    for w in range(CL):
        block = x_ref[:, w * PANELS:(w + 1) * PANELS]
        for zh in range(NZH):
            out_ref[zh, 0, w] = block
    tables = [in_ref[m, SLOTS].astype(F32) for m in range(PEERS)]
    for zh in range(NZH):
        sums = [jnp.zeros((RHS, PANELS), F32) for _ in range(CL)]
        for m in range(PEERS):
            for s in range(zh * CAP, (zh + 1) * CAP):
                block = in_ref[m, s].astype(F32)
                want = jnp.broadcast_to(tables[m][s:s + 1, :], (RHS, PANELS))
                for w in range(CL):
                    sums[w] = sums[w] + jnp.where(want == w, block, 0.0)
        for w in range(CL):
            out_ref[zh, 1, w] = sums[w].astype(BF16)


def near_kernel(near_ref, x_ref, mate_ref, home_ref, *rest):
    got_refs, (blocks_ref, out_ref, region) = rest[:NX - 1], rest[NX - 1:]
    x = lax.axis_index("x")
    c = lax.axis_index("c")
    for w in range(CL):
        region[0, w] = x_ref[:, w * PANELS:(w + 1) * PANELS]
        region[1, w] = mate_ref[0, w]
        total = home_ref[w]
        for k in range(1, NX):
            region[2 * k, w] = got_refs[k - 1][0, w]
            region[2 * k + 1, w] = got_refs[k - 1][1, w]
            total = total + got_refs[k - 1][2, w].astype(F32)
        out_ref[w] = total
    for n in range(NEAR):
        source = near_ref[1, n] % (GRP * CL)
        x_at = source // (NC * CL)
        c_at = (source // CL) % NC
        holder = ((x - x_at + NX) % NX) * NC + (c_at + c) % NC
        out_ref[near_ref[0, n] % CL] += dot_nt(region[holder, source % CL], blocks_ref[n])


def far_kernel(
    far_ref, slot_ref, x_ref, left_ref, right_ref, near_ref, back_ref, out_ref, spread
):
    mask = diagonal_mask()
    total = near_ref[...]
    for z in range(NZH):
        total = total + back_ref[z, 1].astype(F32)
    total = total.reshape(CL * RHS, PANELS)
    spread[...] = jnp.zeros(spread.shape, F32)
    for g in range(GROUPS):
        slots = [slot_ref[g * BATCH + i] for i in range(BATCH)]
        xs = jnp.concatenate([x_ref[s - s // (SLOTS + 1)] for s in slots], axis=0)
        left = left_ref[g * BATCH:(g + 1) * BATCH].reshape(BATCH * RANK, PANELS)
        right = right_ref[g * BATCH:(g + 1) * BATCH].reshape(BATCH * RANK, PANELS)
        coef = jnp.where(mask, dot_nt(xs, right), 0.0)
        for i in range(BATCH):
            target = far_ref[0, g * BATCH + i] % CL
            spread[g, target] += coef[i * RHS:(i + 1) * RHS, :]
        total = total + dot_nn(spread[g].reshape(CL * RHS, PANELS).astype(BF16), left)
    for w in range(CL):
        out_ref[:, w * PANELS:(w + 1) * PANELS] = total[w * RHS:(w + 1) * RHS].astype(BF16)


def shape(dims, dtype=BF16):
    return jax.ShapeDtypeStruct(dims, dtype)


def shift(array, axis, size, by):
    return lax.ppermute(array, axis, [(i, (i + by) % size) for i in range(size)])


def on_device(sources, near_pairs, near_blocks, far_pairs, far_left, far_right):
    near_table = near_pairs.T
    far_table = far_pairs.T
    block = (CL, RHS, PANELS)
    far_send, slots = call(
        far_send_kernel,
        (shape((PEERS * (SLOTS + 1), RHS, PANELS)), shape((FAR,), jnp.int32)),
        [SMEM, ANY, ANY, ANY],
        (ANY, SMEM),
        [
            pltpu.SMEM((NY * NZH * NZL,), jnp.int32),
            pltpu.VMEM((PEERS * SLOTS, PANELS), F32),
            pltpu.VMEM(sources.shape, BF16),
            pltpu.VMEM(far_left.shape, BF16),
            pltpu.VMEM(far_right.shape, BF16),
            pltpu.VMEM((PEERS * (SLOTS + 1), RHS, PANELS), BF16),
            pltpu.SemaphoreType.DMA((4,)),
        ],
        cost=(1000000000, 3500000),
        vmem=60,
    )(far_table, sources, far_left, far_right)
    far_got = lax.all_to_all(
        far_send.reshape(PEERS, SLOTS + 1, RHS, PANELS), ("y", "zl"), 0, 0, tiled=True
    )
    swap, own = call(
        near_send_kernel,
        (shape((1 + NX, *block)), shape((NX, *block), F32)),
        [SMEM, VMEM, VMEM],
        (VMEM, VMEM),
        [pltpu.VMEM((GRP * CL, RHS, PANELS), F32)],
        cost=(1000000000, 3500000),
    )(near_table, sources, near_blocks)
    mate = shift(swap, "c", NC, 1)
    home, *packs = call(
        near_pack_kernel,
        (shape(block, F32),) + (shape((3, *block)),) * (NX - 1),
        [VMEM] * 3,
        (VMEM,) * NX,
        cost=(0, 1000000),
    )(sources, own, mate)
    got = [shift(pack, "x", NX, k + 1) for k, pack in enumerate(packs)]
    near_total = call(
        near_kernel,
        shape(block, F32),
        [SMEM] + [VMEM] * (NX + 3),
        VMEM,
        [pltpu.VMEM((GRP, *block), BF16)],
        cost=(500000000, 2500000),
    )(near_table, sources, mate, home, *got, near_blocks)
    merged = call(
        merge_kernel, shape((NZH, 2, *block)), [VMEM, VMEM], WHOLE, cost=(0, 2000000)
    )(sources, far_got)
    along_z = lax.all_to_all(merged, "zh", 0, 0, tiled=True)
    picked = call(
        pick_kernel,
        shape((PEERS, SLOTS, RHS, PANELS)),
        [VMEM, VMEM, ANY],
        WHOLE,
        cost=(0, 2000000),
    )(along_z, far_got, near_total)
    far_sources = lax.all_to_all(picked, ("y", "zl"), 0, 0, tiled=True)
    return call(
        far_kernel,
        shape(sources.shape),
        [SMEM, SMEM] + [VMEM] * 5,
        VMEM,
        [pltpu.VMEM((GROUPS, *block), F32)],
        cost=(1000000000, 3500000),
    )(
        far_table, slots, far_sources.reshape(PEERS * SLOTS, RHS, PANELS),
        far_left, far_right, near_total, along_z,
    )


def solution(mesh):
    axes = ("y", "zh", "zl", "x", "c")
    fine = Mesh(mesh.devices.reshape(NY, NZH, NZL, NX, NC), axes)
    placed = (
        P(None, axes),
        P(axes, None),
        P(axes, None, None),
        P(axes, None),
        P(axes, None, None),
        P(axes, None, None),
    )
    return jax.shard_map(
        on_device, mesh=fine, in_specs=placed, out_specs=P(None, axes), check_vma=False
    )
```

```python
import jax
import jax.numpy as jnp
from jax import lax
from jax.experimental import pallas as pl
from jax.experimental.pallas import tpu as pltpu
from jax.sharding import Mesh
from jax.sharding import PartitionSpec as P

RHS = 16
PANELS = 256
RANK = 32
LANES = 128
CAP = 2
CL = 4
NY = 4
NZH = 8
NZL = 2
NX = 4
NC = 2
GRP = NX * NC
PEERS = NY * NZL
SLOTS = NZH * CAP
NEAR = 16
FAR = 64
BATCH = 8
GROUPS = FAR // BATCH
ROWS = BATCH * RHS
F32 = jnp.float32
BF16 = jnp.bfloat16

VMEM = pl.BlockSpec(memory_space=pltpu.VMEM)
SMEM = pl.BlockSpec(memory_space=pltpu.SMEM)
ANY = pl.BlockSpec(memory_space=pl.ANY)
WHOLE = pl.BlockSpec()


def call(kernel, out_shape, in_specs, out_specs, scratch=(), cost=(0, 0), vmem=24):
    return pl.pallas_call(
        kernel,
        out_shape=out_shape,
        in_specs=in_specs,
        out_specs=out_specs,
        scratch_shapes=list(scratch),
        compiler_params=pltpu.CompilerParams(vmem_limit_bytes=vmem * 1024 * 1024),
        cost_estimate=pl.CostEstimate(flops=cost[0], bytes_accessed=cost[1], transcendentals=0),
    )


def dot_nt(a, b):
    return lax.dot_general(a, b, (((1,), (1,)), ((), ())), preferred_element_type=F32)


def dot_nn(a, b):
    return lax.dot_general(a, b, (((1,), (0,)), ((), ())), preferred_element_type=F32)


def diagonal_mask():
    row = lax.broadcasted_iota(jnp.int32, (ROWS, PANELS), 0) // RHS
    col = lax.broadcasted_iota(jnp.int32, (ROWS, PANELS), 1) // RANK
    return row == col


def slot_of(source, count):
    owner = source // (GRP * CL)
    order = count[owner]
    count[owner] = order + 1
    y = owner // (NZH * NZL)
    zh = (owner // NZL) % NZH
    zl = owner % NZL
    peer = y * NZL + zl
    return peer, zh * CAP + order


def far_send_kernel(
    far_hbm, x_hbm, left_hbm, right_hbm, out_ref,
    far_ref, count, table, x_ref, left_ref, right_ref, sems,
):
    loads = [
        pltpu.make_async_copy(far_hbm, far_ref, sems.at[0]),
        pltpu.make_async_copy(x_hbm, x_ref, sems.at[1]),
        pltpu.make_async_copy(left_hbm, left_ref, sems.at[2]),
        pltpu.make_async_copy(right_hbm, right_ref, sems.at[3]),
    ]
    for load in loads:
        load.start()
    for o in range(NY * NZH * NZL):
        count[o] = 0
    table[...] = jnp.zeros(table.shape, F32)
    out_ref[...] = jnp.zeros(out_ref.shape, BF16)
    mask = diagonal_mask()
    for load in loads:
        load.wait()
    for g in range(GROUPS):
        slots = []
        for i in range(BATCH):
            source = far_ref[1, g * BATCH + i]
            peer, within = slot_of(source, count)
            slots.append(peer * (SLOTS + 1) + within)
            table[pl.ds(peer * SLOTS + within, 1), :] = jnp.full(
                (1, PANELS), (source % CL).astype(F32)
            )
        targets = [far_ref[0, g * BATCH + i] % CL for i in range(BATCH)]
        xt = jnp.concatenate(
            [x_ref[:, pl.ds(pl.multiple_of(t * PANELS, PANELS), PANELS)] for t in targets], axis=0
        )
        left = left_ref[g * BATCH:(g + 1) * BATCH].reshape(BATCH * RANK, PANELS)
        right = right_ref[g * BATCH:(g + 1) * BATCH].reshape(BATCH * RANK, PANELS)
        coef = jnp.where(mask, dot_nt(xt, left), 0.0).astype(BF16)
        term = dot_nn(coef, right).astype(BF16)
        for i in range(BATCH):
            out_ref[slots[i]] = term[i * RHS:(i + 1) * RHS, :]
    for m in range(PEERS):
        out_ref[m * (SLOTS + 1) + SLOTS] = table[m * SLOTS:(m + 1) * SLOTS, :].astype(BF16)


def near_send_kernel(
    near_ref, far_ref, x_ref, blocks_ref, swap_out, own_out, slot_out, near_sum, count
):
    for o in range(NY * NZH * NZL):
        count[o] = 0
    for n in range(FAR):
        peer, within = slot_of(far_ref[1, n], count)
        slot_out[0, n] = peer * SLOTS + within
        slot_out[1, n] = far_ref[0, n] % CL
    x = lax.axis_index("x")
    c = lax.axis_index("c")
    for w in range(CL):
        swap_out[0, w] = x_ref[:, w * PANELS:(w + 1) * PANELS]
    near_sum[...] = jnp.zeros(near_sum.shape, F32)
    for n in range(NEAR):
        source = near_ref[1, n] % (GRP * CL)
        start = pl.multiple_of((near_ref[0, n] % CL) * PANELS, PANELS)
        near_sum[source] += dot_nn(x_ref[:, pl.ds(start, PANELS)], blocks_ref[n])
    for k in range(NX):
        at = ((x + k) % NX) * (NC * CL)
        own_out[k] = near_sum[pl.ds(at + c * CL, CL)]
        swap_out[1 + k] = near_sum[pl.ds(at + (1 - c) * CL, CL)].astype(BF16)


def near_pack_kernel(x_ref, own_ref, got_ref, home_ref, *out_refs):
    home_ref[...] = own_ref[0] + got_ref[1].astype(F32)
    for k in range(1, NX):
        out = out_refs[k - 1]
        for w in range(CL):
            out[0, w] = x_ref[:, w * PANELS:(w + 1) * PANELS]
        out[1] = got_ref[0]
        out[2] = (own_ref[k] + got_ref[1 + k].astype(F32)).astype(BF16)


def pick_kernel(x_ref, table_ref, after_ref, out_ref):
    def peer(m, _):
        table = table_ref[m, SLOTS].astype(F32)
        for s in range(SLOTS):
            want = jnp.broadcast_to(table[s:s + 1, :], (RHS, PANELS))
            block = x_ref[z_place(s // CAP), 0, 0].astype(F32)
            for w in range(1, CL):
                block = jnp.where(want == w, x_ref[z_place(s // CAP), 0, w].astype(F32), block)
            out_ref[m, s] = block.astype(BF16)
        return 0

    lax.fori_loop(0, PEERS, peer, 0)


def z_place(zh):
    return NZH - 1 - zh


def merge_kernel(x_ref, in_ref, out_hbm, out_ref, table, sems):
    for w in range(CL):
        block = x_ref[:, w * PANELS:(w + 1) * PANELS]
        for zh in range(NZH):
            out_ref[zh, 0, w] = block
    for m in range(PEERS):
        table[m] = in_ref[m, SLOTS][:, :LANES].astype(F32)
    stores = []
    for zh in range(NZH):
        at = z_place(zh)
        for h in range(PANELS // LANES):
            lanes = slice(h * LANES, (h + 1) * LANES)
            sums = [jnp.zeros((2, RHS // 2, LANES), F32) for _ in range(CL)]
            for m in range(PEERS):
                for s in range(zh * CAP, (zh + 1) * CAP):
                    block = in_ref[m, s, :, lanes].astype(F32).reshape(2, RHS // 2, LANES)
                    want = jnp.broadcast_to(table[m, s:s + 1, :], (RHS // 2, LANES))
                    for w in range(CL):
                        sums[w] = sums[w] + jnp.where((want == w)[None], block, 0.0)
            for w in range(CL):
                out_ref[at, 1, w, :, lanes] = sums[w].reshape(RHS, LANES).astype(BF16)
        stores.append(pltpu.make_async_copy(out_ref.at[at], out_hbm.at[at], sems.at[at]))
        stores[-1].start()
    for store in stores:
        store.wait()


def near_kernel(near_ref, x_ref, mate_ref, home_ref, *rest):
    got_refs, (blocks_ref, out_ref, region) = rest[:NX - 1], rest[NX - 1:]
    x = lax.axis_index("x")
    c = lax.axis_index("c")
    for w in range(CL):
        region[0, w] = x_ref[:, w * PANELS:(w + 1) * PANELS]
        region[1, w] = mate_ref[0, w]
        total = home_ref[w]
        for k in range(1, NX):
            region[2 * k, w] = got_refs[k - 1][0, w]
            region[2 * k + 1, w] = got_refs[k - 1][1, w]
            total = total + got_refs[k - 1][2, w].astype(F32)
        out_ref[w] = total
    for n in range(NEAR):
        source = near_ref[1, n] % (GRP * CL)
        x_at = source // (NC * CL)
        c_at = (source // CL) % NC
        holder = ((x - x_at + NX) % NX) * NC + (c_at + c) % NC
        out_ref[near_ref[0, n] % CL] += dot_nt(region[holder, source % CL], blocks_ref[n])


def far_kernel(
    slot_ref, x_ref, left_ref, right_ref, near_ref, back_ref, out_ref, spread
):
    mask = diagonal_mask()
    total = near_ref[...]
    for z in range(NZH):
        total = total + back_ref[z, 1].astype(F32)
    total = total.reshape(CL * RHS, PANELS)
    spread[...] = jnp.zeros(spread.shape, F32)
    for g in range(GROUPS):
        xs = jnp.concatenate([x_ref[slot_ref[0, g * BATCH + i]] for i in range(BATCH)], axis=0)
        left = left_ref[g * BATCH:(g + 1) * BATCH].reshape(BATCH * RANK, PANELS)
        right = right_ref[g * BATCH:(g + 1) * BATCH].reshape(BATCH * RANK, PANELS)
        coef = jnp.where(mask, dot_nt(xs, right), 0.0)
        for i in range(BATCH):
            spread[g, slot_ref[1, g * BATCH + i]] += coef[i * RHS:(i + 1) * RHS, :]
        total = total + dot_nn(spread[g].reshape(CL * RHS, PANELS).astype(BF16), left)
    for w in range(CL):
        out_ref[:, w * PANELS:(w + 1) * PANELS] = total[w * RHS:(w + 1) * RHS].astype(BF16)


def shape(dims, dtype=BF16):
    return jax.ShapeDtypeStruct(dims, dtype)


def shift(array, axis, size, by):
    return lax.ppermute(array, axis, [(i, (i + by) % size) for i in range(size)])


def on_device(sources, near_pairs, near_blocks, far_pairs, far_left, far_right):
    near_table = near_pairs.T
    far_table = far_pairs.T
    block = (CL, RHS, PANELS)
    far_send = call(
        far_send_kernel,
        shape((PEERS * (SLOTS + 1), RHS, PANELS)),
        [ANY] * 4,
        VMEM,
        [
            pltpu.SMEM(far_table.shape, jnp.int32),
            pltpu.SMEM((NY * NZH * NZL,), jnp.int32),
            pltpu.VMEM((PEERS * SLOTS, PANELS), F32),
            pltpu.VMEM(sources.shape, BF16),
            pltpu.VMEM(far_left.shape, BF16),
            pltpu.VMEM(far_right.shape, BF16),
            pltpu.SemaphoreType.DMA((4,)),
        ],
        cost=(1000000000, 3500000),
        vmem=58,
    )(far_table, sources, far_left, far_right)
    far_got = lax.all_to_all(
        far_send.reshape(PEERS, SLOTS + 1, RHS, PANELS), ("y", "e"), 0, 0, tiled=True
    )
    swap, own, slots = call(
        near_send_kernel,
        (shape((1 + NX, *block)), shape((NX, *block), F32), shape((2, FAR), jnp.int32)),
        [SMEM, SMEM, VMEM, VMEM],
        (VMEM, VMEM, SMEM),
        [
            pltpu.VMEM((GRP * CL, RHS, PANELS), F32),
            pltpu.SMEM((NY * NZH * NZL,), jnp.int32),
        ],
        cost=(1000000000, 3500000),
    )(near_table, far_table, sources, near_blocks)
    mate = shift(swap, "c", NC, 1)
    home, *packs = call(
        near_pack_kernel,
        (shape(block, F32),) + (shape((3, *block)),) * (NX - 1),
        [VMEM] * 3,
        (VMEM,) * NX,
        cost=(0, 1000000),
    )(sources, own, mate)
    got = [shift(pack, "x", NX, k + 1) for k, pack in enumerate(packs)]
    near_total = call(
        near_kernel,
        shape(block, F32),
        [SMEM] + [VMEM] * (NX + 3),
        VMEM,
        [pltpu.VMEM((GRP, *block), BF16)],
        cost=(500000000, 2500000),
    )(near_table, sources, mate, home, *got, near_blocks)
    merged = call(
        merge_kernel,
        shape((NZH, 2, *block)),
        [VMEM, VMEM],
        ANY,
        [
            pltpu.VMEM((NZH, 2, *block), BF16),
            pltpu.VMEM((PEERS, SLOTS, LANES), F32),
            pltpu.SemaphoreType.DMA((NZH,)),
        ],
        cost=(0, 2000000),
    )(sources, far_got)
    along_z = lax.all_to_all(
        merged, "zh", 0, 0, axis_index_groups=[list(range(NZH))[::-1]], tiled=True
    )
    picked = call(
        pick_kernel,
        shape((PEERS, SLOTS, RHS, PANELS)),
        [VMEM, VMEM, ANY],
        WHOLE,
        cost=(0, 2000000),
    )(along_z, far_got, near_total)
    far_sources = lax.all_to_all(picked, ("y", "e"), 0, 0, tiled=True)
    return call(
        far_kernel,
        shape(sources.shape),
        [SMEM] + [VMEM] * 5,
        VMEM,
        [pltpu.VMEM((GROUPS, *block), F32)],
        cost=(1000000000, 3500000),
    )(
        slots, far_sources.reshape(PEERS * SLOTS, RHS, PANELS),
        far_left, far_right, near_total, along_z,
    )


def solution(mesh):
    axes = ("y", "zh", "e", "x", "c")
    fine = Mesh(mesh.devices.reshape(NY, NZH, NZL, NX, NC), axes)
    placed = (
        P(None, axes),
        P(axes, None),
        P(axes, None, None),
        P(axes, None),
        P(axes, None, None),
        P(axes, None, None),
    )
    return jax.shard_map(
        on_device, mesh=fine, in_specs=placed, out_specs=P(None, axes), check_vma=False
    )
```

```python
import jax
import jax.numpy as jnp
from jax import lax
from jax.experimental import pallas as pl
from jax.experimental.pallas import tpu as pltpu
from jax.sharding import Mesh
from jax.sharding import PartitionSpec as P

RHS = 16
PANELS = 256
RANK = 32
LANES = 128
CAP = 2
CL = 4
NY = 4
NZH = 8
NZL = 2
NX = 4
NC = 2
GRP = NX * NC
PEERS = NY * NZL
SLOTS = NZH * CAP
NEAR = 16
FAR = 64
BATCH = 8
GROUPS = FAR // BATCH
PARTS = 4
ROWS = BATCH * RHS
F32 = jnp.float32
BF16 = jnp.bfloat16

VMEM = pl.BlockSpec(memory_space=pltpu.VMEM)
SMEM = pl.BlockSpec(memory_space=pltpu.SMEM)
ANY = pl.BlockSpec(memory_space=pl.ANY)
WHOLE = pl.BlockSpec()


def call(kernel, out_shape, in_specs, out_specs, scratch=(), cost=(0, 0), vmem=24):
    return pl.pallas_call(
        kernel,
        out_shape=out_shape,
        in_specs=in_specs,
        out_specs=out_specs,
        scratch_shapes=list(scratch),
        compiler_params=pltpu.CompilerParams(vmem_limit_bytes=vmem * 1024 * 1024),
        cost_estimate=pl.CostEstimate(flops=cost[0], bytes_accessed=cost[1], transcendentals=0),
    )


def dot_nt(a, b):
    return lax.dot_general(a, b, (((1,), (1,)), ((), ())), preferred_element_type=F32)


def dot_nn(a, b):
    return lax.dot_general(a, b, (((1,), (0,)), ((), ())), preferred_element_type=F32)


def diagonal_mask():
    row = lax.broadcasted_iota(jnp.int32, (ROWS, PANELS), 0) // RHS
    col = lax.broadcasted_iota(jnp.int32, (ROWS, PANELS), 1) // RANK
    return row == col


def slot_of(source, count):
    owner = source // (GRP * CL)
    order = count[owner]
    count[owner] = order + 1
    y = owner // (NZH * NZL)
    zh = (owner // NZL) % NZH
    zl = owner % NZL
    peer = y * NZL + zl
    return peer, zh * CAP + order


def far_send_kernel(
    far_hbm, x_hbm, left_hbm, right_hbm, out_ref,
    far_ref, count, table, x_ref, left_ref, right_ref, sems,
):
    loads = [
        pltpu.make_async_copy(far_hbm, far_ref, sems.at[0]),
        pltpu.make_async_copy(x_hbm, x_ref, sems.at[1]),
    ]
    for p in range(PARTS):
        pairs = pl.ds(p * (FAR // PARTS), FAR // PARTS)
        for i, (hbm, ref) in enumerate(((left_hbm, left_ref), (right_hbm, right_ref))):
            loads.append(
                pltpu.make_async_copy(hbm.at[pairs], ref.at[pairs], sems.at[2 + 2 * p + i])
            )
    for load in loads:
        load.start()
    for o in range(NY * NZH * NZL):
        count[o] = 0
    table[...] = jnp.zeros(table.shape, F32)
    out_ref[...] = jnp.zeros(out_ref.shape, BF16)
    mask = diagonal_mask()
    loads[0].wait()
    loads[1].wait()
    for g in range(GROUPS):
        if g % (GROUPS // PARTS) == 0:
            part = g // (GROUPS // PARTS)
            loads[2 + 2 * part].wait()
            loads[3 + 2 * part].wait()
        slots = []
        for i in range(BATCH):
            source = far_ref[1, g * BATCH + i]
            peer, within = slot_of(source, count)
            slots.append(peer * (SLOTS + 1) + within)
            table[pl.ds(peer * SLOTS + within, 1), :] = jnp.full(
                (1, PANELS), (source % CL).astype(F32)
            )
        targets = [far_ref[0, g * BATCH + i] % CL for i in range(BATCH)]
        xt = jnp.concatenate(
            [x_ref[:, pl.ds(pl.multiple_of(t * PANELS, PANELS), PANELS)] for t in targets], axis=0
        )
        left = left_ref[g * BATCH:(g + 1) * BATCH].reshape(BATCH * RANK, PANELS)
        right = right_ref[g * BATCH:(g + 1) * BATCH].reshape(BATCH * RANK, PANELS)
        coef = jnp.where(mask, dot_nt(xt, left), 0.0).astype(BF16)
        term = dot_nn(coef, right).astype(BF16)
        for i in range(BATCH):
            out_ref[slots[i]] = term[i * RHS:(i + 1) * RHS, :]
    for m in range(PEERS):
        out_ref[m * (SLOTS + 1) + SLOTS] = table[m * SLOTS:(m + 1) * SLOTS, :].astype(BF16)


def near_send_kernel(
    near_ref, far_ref, x_ref, blocks_ref, swap_out, own_out, slot_out, near_sum, count
):
    for o in range(NY * NZH * NZL):
        count[o] = 0
    for n in range(FAR):
        peer, within = slot_of(far_ref[1, n], count)
        slot_out[0, n] = peer * SLOTS + within
        slot_out[1, n] = far_ref[0, n] % CL
    x = lax.axis_index("x")
    c = lax.axis_index("c")
    for w in range(CL):
        swap_out[0, w] = x_ref[:, w * PANELS:(w + 1) * PANELS]
    near_sum[...] = jnp.zeros(near_sum.shape, F32)
    for n in range(NEAR):
        source = near_ref[1, n] % (GRP * CL)
        start = pl.multiple_of((near_ref[0, n] % CL) * PANELS, PANELS)
        near_sum[source] += dot_nn(x_ref[:, pl.ds(start, PANELS)], blocks_ref[n])
    for k in range(NX):
        at = ((x + k) % NX) * (NC * CL)
        own_out[k] = near_sum[pl.ds(at + c * CL, CL)]
        swap_out[1 + k] = near_sum[pl.ds(at + (1 - c) * CL, CL)].astype(BF16)


def near_pack_kernel(x_ref, own_ref, got_ref, home_ref, *out_refs):
    home_ref[...] = own_ref[0] + got_ref[1].astype(F32)
    for k in range(1, NX):
        out = out_refs[k - 1]
        for w in range(CL):
            out[0, w] = x_ref[:, w * PANELS:(w + 1) * PANELS]
        out[1] = got_ref[0]
        out[2] = (own_ref[k] + got_ref[1 + k].astype(F32)).astype(BF16)


def pick_kernel(x_ref, table_ref, after_ref, out_ref):
    def peer(m, _):
        table = table_ref[m, SLOTS].astype(F32)
        for s in range(SLOTS):
            want = jnp.broadcast_to(table[s:s + 1, :], (RHS, PANELS))
            block = x_ref[z_place(s // CAP), 0, 0].astype(F32)
            for w in range(1, CL):
                block = jnp.where(want == w, x_ref[z_place(s // CAP), 0, w].astype(F32), block)
            out_ref[m, s] = block.astype(BF16)
        return 0

    lax.fori_loop(0, PEERS, peer, 0)


def z_place(zh):
    return NZH - 1 - zh


def merge_kernel(x_ref, in_ref, out_hbm, out_ref, table, sems):
    for w in range(CL):
        block = x_ref[:, w * PANELS:(w + 1) * PANELS]
        for zh in range(NZH):
            out_ref[zh, 0, w] = block
    for m in range(PEERS):
        table[m] = in_ref[m, SLOTS][:, :LANES].astype(F32)
    stores = []
    for zh in range(NZH):
        at = z_place(zh)
        for h in range(PANELS // LANES):
            lanes = slice(h * LANES, (h + 1) * LANES)
            sums = [jnp.zeros((2, RHS // 2, LANES), F32) for _ in range(CL)]
            for m in range(PEERS):
                for s in range(zh * CAP, (zh + 1) * CAP):
                    block = in_ref[m, s, :, lanes].astype(F32).reshape(2, RHS // 2, LANES)
                    want = jnp.broadcast_to(table[m, s:s + 1, :], (RHS // 2, LANES))
                    for w in range(CL):
                        sums[w] = sums[w] + jnp.where((want == w)[None], block, 0.0)
            for w in range(CL):
                out_ref[at, 1, w, :, lanes] = sums[w].reshape(RHS, LANES).astype(BF16)
        stores.append(pltpu.make_async_copy(out_ref.at[at], out_hbm.at[at], sems.at[at]))
        stores[-1].start()
    for store in stores:
        store.wait()


def near_kernel(near_ref, x_ref, mate_ref, home_ref, *rest):
    got_refs, (blocks_ref, out_ref, region) = rest[:NX - 1], rest[NX - 1:]
    x = lax.axis_index("x")
    c = lax.axis_index("c")
    for w in range(CL):
        region[0, w] = x_ref[:, w * PANELS:(w + 1) * PANELS]
        region[1, w] = mate_ref[0, w]
        total = home_ref[w]
        for k in range(1, NX):
            region[2 * k, w] = got_refs[k - 1][0, w]
            region[2 * k + 1, w] = got_refs[k - 1][1, w]
            total = total + got_refs[k - 1][2, w].astype(F32)
        out_ref[w] = total
    for n in range(NEAR):
        source = near_ref[1, n] % (GRP * CL)
        x_at = source // (NC * CL)
        c_at = (source // CL) % NC
        holder = ((x - x_at + NX) % NX) * NC + (c_at + c) % NC
        out_ref[near_ref[0, n] % CL] += dot_nt(region[holder, source % CL], blocks_ref[n])


def far_kernel(
    slot_ref, x_ref, left_ref, right_ref, near_ref, back_ref, out_ref, spread
):
    mask = diagonal_mask()
    total = near_ref[...]
    for z in range(NZH):
        total = total + back_ref[z, 1].astype(F32)
    total = total.reshape(CL * RHS, PANELS)
    spread[...] = jnp.zeros(spread.shape, F32)
    for g in range(GROUPS):
        xs = jnp.concatenate([x_ref[slot_ref[0, g * BATCH + i]] for i in range(BATCH)], axis=0)
        left = left_ref[g * BATCH:(g + 1) * BATCH].reshape(BATCH * RANK, PANELS)
        right = right_ref[g * BATCH:(g + 1) * BATCH].reshape(BATCH * RANK, PANELS)
        coef = jnp.where(mask, dot_nt(xs, right), 0.0)
        for i in range(BATCH):
            spread[g, slot_ref[1, g * BATCH + i]] += coef[i * RHS:(i + 1) * RHS, :]
        total = total + dot_nn(spread[g].reshape(CL * RHS, PANELS).astype(BF16), left)
    for w in range(CL):
        out_ref[:, w * PANELS:(w + 1) * PANELS] = total[w * RHS:(w + 1) * RHS].astype(BF16)


def shape(dims, dtype=BF16):
    return jax.ShapeDtypeStruct(dims, dtype)


def shift(array, axis, size, by):
    return lax.ppermute(array, axis, [(i, (i + by) % size) for i in range(size)])


def on_device(sources, near_pairs, near_blocks, far_pairs, far_left, far_right):
    near_table = near_pairs.T
    far_table = far_pairs.T
    block = (CL, RHS, PANELS)
    far_send = call(
        far_send_kernel,
        shape((PEERS * (SLOTS + 1), RHS, PANELS)),
        [ANY] * 4,
        VMEM,
        [
            pltpu.SMEM(far_table.shape, jnp.int32),
            pltpu.SMEM((NY * NZH * NZL,), jnp.int32),
            pltpu.VMEM((PEERS * SLOTS, PANELS), F32),
            pltpu.VMEM(sources.shape, BF16),
            pltpu.VMEM(far_left.shape, BF16),
            pltpu.VMEM(far_right.shape, BF16),
            pltpu.SemaphoreType.DMA((2 + 2 * PARTS,)),
        ],
        cost=(1000000000, 3500000),
        vmem=58,
    )(far_table, sources, far_left, far_right)
    far_got = lax.all_to_all(
        far_send.reshape(PEERS, SLOTS + 1, RHS, PANELS), ("y", "e"), 0, 0, tiled=True
    )
    swap, own, slots = call(
        near_send_kernel,
        (shape((1 + NX, *block)), shape((NX, *block), F32), shape((2, FAR), jnp.int32)),
        [SMEM, SMEM, VMEM, VMEM],
        (VMEM, VMEM, SMEM),
        [
            pltpu.VMEM((GRP * CL, RHS, PANELS), F32),
            pltpu.SMEM((NY * NZH * NZL,), jnp.int32),
        ],
        cost=(1000000000, 3500000),
    )(near_table, far_table, sources, near_blocks)
    mate = shift(swap, "c", NC, 1)
    home, *packs = call(
        near_pack_kernel,
        (shape(block, F32),) + (shape((3, *block)),) * (NX - 1),
        [VMEM] * 3,
        (VMEM,) * NX,
        cost=(0, 1000000),
    )(sources, own, mate)
    got = [shift(pack, "x", NX, k + 1) for k, pack in enumerate(packs)]
    near_total = call(
        near_kernel,
        shape(block, F32),
        [SMEM] + [VMEM] * (NX + 3),
        VMEM,
        [pltpu.VMEM((GRP, *block), BF16)],
        cost=(500000000, 2500000),
    )(near_table, sources, mate, home, *got, near_blocks)
    merged = call(
        merge_kernel,
        shape((NZH, 2, *block)),
        [VMEM, VMEM],
        ANY,
        [
            pltpu.VMEM((NZH, 2, *block), BF16),
            pltpu.VMEM((PEERS, SLOTS, LANES), F32),
            pltpu.SemaphoreType.DMA((NZH,)),
        ],
        cost=(0, 2000000),
    )(sources, far_got)
    along_z = lax.all_to_all(
        merged, "zh", 0, 0, axis_index_groups=[list(range(NZH))[::-1]], tiled=True
    )
    picked = call(
        pick_kernel,
        shape((PEERS, SLOTS, RHS, PANELS)),
        [VMEM, VMEM, ANY],
        WHOLE,
        cost=(0, 2000000),
    )(along_z, far_got, near_total)
    far_sources = lax.all_to_all(picked, ("y", "e"), 0, 0, tiled=True)
    return call(
        far_kernel,
        shape(sources.shape),
        [SMEM] + [VMEM] * 5,
        VMEM,
        [pltpu.VMEM((GROUPS, *block), F32)],
        cost=(1000000000, 3500000),
    )(
        slots, far_sources.reshape(PEERS * SLOTS, RHS, PANELS),
        far_left, far_right, near_total, along_z,
    )


def solution(mesh):
    axes = ("y", "zh", "e", "x", "c")
    fine = Mesh(mesh.devices.reshape(NY, NZH, NZL, NX, NC), axes)
    placed = (
        P(None, axes),
        P(axes, None),
        P(axes, None, None),
        P(axes, None),
        P(axes, None, None),
        P(axes, None, None),
    )
    return jax.shard_map(
        on_device, mesh=fine, in_specs=placed, out_specs=P(None, axes), check_vma=False
    )
```

```python
import jax
import jax.numpy as jnp
from jax import lax
from jax.experimental import pallas as pl
from jax.experimental.pallas import tpu as pltpu
from jax.sharding import Mesh
from jax.sharding import PartitionSpec as P

RHS = 16
PANELS = 256
RANK = 32
LANES = 128
CAP = 2
CL = 4
NY = 4
NZH = 8
NZL = 2
NX = 4
NC = 2
GRP = NX * NC
PEERS = NY * NZL
SLOTS = NZH * CAP
NEAR = 16
FAR = 64
BATCH = 8
GROUPS = FAR // BATCH
ROWS = BATCH * RHS
F32 = jnp.float32
BF16 = jnp.bfloat16

VMEM = pl.BlockSpec(memory_space=pltpu.VMEM)
SMEM = pl.BlockSpec(memory_space=pltpu.SMEM)
ANY = pl.BlockSpec(memory_space=pl.ANY)
WHOLE = pl.BlockSpec()


def call(kernel, out_shape, in_specs, out_specs, scratch=(), cost=(0, 0), vmem=24):
    return pl.pallas_call(
        kernel,
        out_shape=out_shape,
        in_specs=in_specs,
        out_specs=out_specs,
        scratch_shapes=list(scratch),
        compiler_params=pltpu.CompilerParams(vmem_limit_bytes=vmem * 1024 * 1024),
        cost_estimate=pl.CostEstimate(flops=cost[0], bytes_accessed=cost[1], transcendentals=0),
    )


def dot_nt(a, b):
    return lax.dot_general(a, b, (((1,), (1,)), ((), ())), preferred_element_type=F32)


def dot_nn(a, b):
    return lax.dot_general(a, b, (((1,), (0,)), ((), ())), preferred_element_type=F32)


def diagonal_mask():
    row = lax.broadcasted_iota(jnp.int32, (ROWS, PANELS), 0) // RHS
    col = lax.broadcasted_iota(jnp.int32, (ROWS, PANELS), 1) // RANK
    return row == col


def quotient(value, power):
    return value >> (power.bit_length() - 1)


def remainder(value, power):
    return value & (power - 1)


def slot_of(source, count):
    owner = quotient(source, GRP * CL)
    order = count[owner]
    count[owner] = order + 1
    y = quotient(owner, NZH * NZL)
    zh = remainder(quotient(owner, NZL), NZH)
    zl = remainder(owner, NZL)
    peer = y * NZL + zl
    return peer, zh * CAP + order


def far_send_kernel(
    far_hbm, x_hbm, left_hbm, right_hbm, out_ref,
    far_ref, count, table, x_ref, left_ref, right_ref, sems,
):
    loads = [
        pltpu.make_async_copy(far_hbm, far_ref, sems.at[0]),
        pltpu.make_async_copy(x_hbm, x_ref, sems.at[1]),
        pltpu.make_async_copy(left_hbm, left_ref, sems.at[2]),
        pltpu.make_async_copy(right_hbm, right_ref, sems.at[3]),
    ]
    for load in loads:
        load.start()
    for o in range(NY * NZH * NZL):
        count[o] = 0
    table[...] = jnp.zeros(table.shape, F32)
    out_ref[...] = jnp.zeros(out_ref.shape, BF16)
    mask = diagonal_mask()
    for load in loads:
        load.wait()
    for g in range(GROUPS):
        slots = []
        for i in range(BATCH):
            source = far_ref[1, g * BATCH + i]
            peer, within = slot_of(source, count)
            slots.append(peer * (SLOTS + 1) + within)
            table[pl.ds(peer * SLOTS + within, 1), :] = jnp.full(
                (1, PANELS), remainder(source, CL).astype(F32)
            )
        targets = [remainder(far_ref[0, g * BATCH + i], CL) for i in range(BATCH)]
        xt = jnp.concatenate(
            [x_ref[:, pl.ds(pl.multiple_of(t * PANELS, PANELS), PANELS)] for t in targets], axis=0
        )
        left = left_ref[g * BATCH:(g + 1) * BATCH].reshape(BATCH * RANK, PANELS)
        right = right_ref[g * BATCH:(g + 1) * BATCH].reshape(BATCH * RANK, PANELS)
        coef = jnp.where(mask, dot_nt(xt, left), 0.0).astype(BF16)
        term = dot_nn(coef, right).astype(BF16)
        for i in range(BATCH):
            out_ref[slots[i]] = term[i * RHS:(i + 1) * RHS, :]
    for m in range(PEERS):
        out_ref[m * (SLOTS + 1) + SLOTS] = table[m * SLOTS:(m + 1) * SLOTS, :].astype(BF16)


def near_send_kernel(
    near_ref, far_ref, x_ref, blocks_ref, swap_out, own_out, slot_out, near_sum, count
):
    for o in range(NY * NZH * NZL):
        count[o] = 0
    for n in range(FAR):
        peer, within = slot_of(far_ref[1, n], count)
        slot_out[0, n] = peer * SLOTS + within
        slot_out[1, n] = remainder(far_ref[0, n], CL)
    x = lax.axis_index("x")
    c = lax.axis_index("c")
    for w in range(CL):
        swap_out[0, w] = x_ref[:, w * PANELS:(w + 1) * PANELS]
    near_sum[...] = jnp.zeros(near_sum.shape, F32)
    for n in range(NEAR):
        source = remainder(near_ref[1, n], GRP * CL)
        start = pl.multiple_of((remainder(near_ref[0, n], CL)) * PANELS, PANELS)
        near_sum[source] += dot_nn(x_ref[:, pl.ds(start, PANELS)], blocks_ref[n])
    for k in range(NX):
        at = ((x + k) % NX) * (NC * CL)
        own_out[k] = near_sum[pl.ds(at + c * CL, CL)]
        swap_out[1 + k] = near_sum[pl.ds(at + (1 - c) * CL, CL)].astype(BF16)


def near_pack_kernel(x_ref, own_ref, got_ref, home_ref, *out_refs):
    home_ref[...] = own_ref[0] + got_ref[1].astype(F32)
    for k in range(1, NX):
        out = out_refs[k - 1]
        for w in range(CL):
            out[0, w] = x_ref[:, w * PANELS:(w + 1) * PANELS]
        out[1] = got_ref[0]
        out[2] = (own_ref[k] + got_ref[1 + k].astype(F32)).astype(BF16)


def pick_kernel(x_ref, table_ref, after_ref, out_ref):
    def peer(m, _):
        table = table_ref[m, SLOTS].astype(F32)
        for s in range(SLOTS):
            want = jnp.broadcast_to(table[s:s + 1, :], (RHS, PANELS))
            block = x_ref[z_place(s // CAP), 0, 0].astype(F32)
            for w in range(1, CL):
                block = jnp.where(want == w, x_ref[z_place(s // CAP), 0, w].astype(F32), block)
            out_ref[m, s] = block.astype(BF16)
        return 0

    lax.fori_loop(0, PEERS, peer, 0)


def z_place(zh):
    return NZH - 1 - zh


def merge_kernel(x_ref, in_ref, out_hbm, out_ref, table, sems):
    for w in range(CL):
        block = x_ref[:, w * PANELS:(w + 1) * PANELS]
        for zh in range(NZH):
            out_ref[zh, 0, w] = block
    for m in range(PEERS):
        table[m] = in_ref[m, SLOTS][:, :LANES].astype(F32)
    stores = []
    for zh in range(NZH):
        at = z_place(zh)
        for h in range(PANELS // LANES):
            lanes = slice(h * LANES, (h + 1) * LANES)
            sums = [jnp.zeros((2, RHS // 2, LANES), F32) for _ in range(CL)]
            for m in range(PEERS):
                for s in range(zh * CAP, (zh + 1) * CAP):
                    block = in_ref[m, s, :, lanes].astype(F32).reshape(2, RHS // 2, LANES)
                    want = jnp.broadcast_to(table[m, s:s + 1, :], (RHS // 2, LANES))
                    for w in range(CL):
                        sums[w] = sums[w] + jnp.where((want == w)[None], block, 0.0)
            for w in range(CL):
                out_ref[at, 1, w, :, lanes] = sums[w].reshape(RHS, LANES).astype(BF16)
        stores.append(pltpu.make_async_copy(out_ref.at[at], out_hbm.at[at], sems.at[at]))
        stores[-1].start()
    for store in stores:
        store.wait()


def near_kernel(near_ref, x_ref, mate_ref, home_ref, *rest):
    got_refs, (blocks_ref, out_ref, region) = rest[:NX - 1], rest[NX - 1:]
    x = lax.axis_index("x")
    c = lax.axis_index("c")
    for w in range(CL):
        region[0, w] = x_ref[:, w * PANELS:(w + 1) * PANELS]
        region[1, w] = mate_ref[0, w]
        total = home_ref[w]
        for k in range(1, NX):
            region[2 * k, w] = got_refs[k - 1][0, w]
            region[2 * k + 1, w] = got_refs[k - 1][1, w]
            total = total + got_refs[k - 1][2, w].astype(F32)
        out_ref[w] = total
    for n in range(NEAR):
        source = remainder(near_ref[1, n], GRP * CL)
        x_at = quotient(source, NC * CL)
        c_at = remainder(quotient(source, CL), NC)
        holder = remainder(x - x_at + NX, NX) * NC + remainder(c_at + c, NC)
        out_ref[remainder(near_ref[0, n], CL)] += dot_nt(region[holder, remainder(source, CL)], blocks_ref[n])


def far_kernel(
    slot_ref, x_ref, left_ref, right_ref, near_ref, back_ref, out_ref, spread
):
    mask = diagonal_mask()
    total = near_ref[...]
    for z in range(NZH):
        total = total + back_ref[z, 1].astype(F32)
    total = total.reshape(CL * RHS, PANELS)
    spread[...] = jnp.zeros(spread.shape, F32)
    for g in range(GROUPS):
        xs = jnp.concatenate([x_ref[slot_ref[0, g * BATCH + i]] for i in range(BATCH)], axis=0)
        left = left_ref[g * BATCH:(g + 1) * BATCH].reshape(BATCH * RANK, PANELS)
        right = right_ref[g * BATCH:(g + 1) * BATCH].reshape(BATCH * RANK, PANELS)
        coef = jnp.where(mask, dot_nt(xs, right), 0.0)
        for i in range(BATCH):
            spread[g, slot_ref[1, g * BATCH + i]] += coef[i * RHS:(i + 1) * RHS, :]
        total = total + dot_nn(spread[g].reshape(CL * RHS, PANELS).astype(BF16), left)
    for w in range(CL):
        out_ref[:, w * PANELS:(w + 1) * PANELS] = total[w * RHS:(w + 1) * RHS].astype(BF16)


def shape(dims, dtype=BF16):
    return jax.ShapeDtypeStruct(dims, dtype)


def shift(array, axis, size, by):
    return lax.ppermute(array, axis, [(i, (i + by) % size) for i in range(size)])


def on_device(sources, near_pairs, near_blocks, far_pairs, far_left, far_right):
    near_table = near_pairs.T
    far_table = far_pairs.T
    block = (CL, RHS, PANELS)
    far_send = call(
        far_send_kernel,
        shape((PEERS * (SLOTS + 1), RHS, PANELS)),
        [ANY] * 4,
        VMEM,
        [
            pltpu.SMEM(far_table.shape, jnp.int32),
            pltpu.SMEM((NY * NZH * NZL,), jnp.int32),
            pltpu.VMEM((PEERS * SLOTS, PANELS), F32),
            pltpu.VMEM(sources.shape, BF16),
            pltpu.VMEM(far_left.shape, BF16),
            pltpu.VMEM(far_right.shape, BF16),
            pltpu.SemaphoreType.DMA((4,)),
        ],
        cost=(1000000000, 3500000),
        vmem=58,
    )(far_table, sources, far_left, far_right)
    far_got = lax.all_to_all(
        far_send.reshape(PEERS, SLOTS + 1, RHS, PANELS), ("y", "e"), 0, 0, tiled=True
    )
    swap, own, slots = call(
        near_send_kernel,
        (shape((1 + NX, *block)), shape((NX, *block), F32), shape((2, FAR), jnp.int32)),
        [SMEM, SMEM, VMEM, VMEM],
        (VMEM, VMEM, SMEM),
        [
            pltpu.VMEM((GRP * CL, RHS, PANELS), F32),
            pltpu.SMEM((NY * NZH * NZL,), jnp.int32),
        ],
        cost=(1000000000, 3500000),
    )(near_table, far_table, sources, near_blocks)
    mate = shift(swap, "c", NC, 1)
    home, *packs = call(
        near_pack_kernel,
        (shape(block, F32),) + (shape((3, *block)),) * (NX - 1),
        [VMEM] * 3,
        (VMEM,) * NX,
        cost=(0, 1000000),
    )(sources, own, mate)
    got = [shift(pack, "x", NX, k + 1) for k, pack in enumerate(packs)]
    near_total = call(
        near_kernel,
        shape(block, F32),
        [SMEM] + [VMEM] * (NX + 3),
        VMEM,
        [pltpu.VMEM((GRP, *block), BF16)],
        cost=(500000000, 2500000),
    )(near_table, sources, mate, home, *got, near_blocks)
    merged = call(
        merge_kernel,
        shape((NZH, 2, *block)),
        [VMEM, VMEM],
        ANY,
        [
            pltpu.VMEM((NZH, 2, *block), BF16),
            pltpu.VMEM((PEERS, SLOTS, LANES), F32),
            pltpu.SemaphoreType.DMA((NZH,)),
        ],
        cost=(0, 2000000),
    )(sources, far_got)
    along_z = lax.all_to_all(
        merged, "zh", 0, 0, axis_index_groups=[list(range(NZH))[::-1]], tiled=True
    )
    picked = call(
        pick_kernel,
        shape((PEERS, SLOTS, RHS, PANELS)),
        [VMEM, VMEM, ANY],
        WHOLE,
        cost=(0, 2000000),
    )(along_z, far_got, near_total)
    far_sources = lax.all_to_all(picked, ("y", "e"), 0, 0, tiled=True)
    return call(
        far_kernel,
        shape(sources.shape),
        [SMEM] + [VMEM] * 5,
        VMEM,
        [pltpu.VMEM((GROUPS, *block), F32)],
        cost=(1000000000, 3500000),
    )(
        slots, far_sources.reshape(PEERS * SLOTS, RHS, PANELS),
        far_left, far_right, near_total, along_z,
    )


def solution(mesh):
    axes = ("y", "zh", "e", "x", "c")
    fine = Mesh(mesh.devices.reshape(NY, NZH, NZL, NX, NC), axes)
    placed = (
        P(None, axes),
        P(axes, None),
        P(axes, None, None),
        P(axes, None),
        P(axes, None, None),
        P(axes, None, None),
    )
    return jax.shard_map(
        on_device, mesh=fine, in_specs=placed, out_specs=P(None, axes), check_vma=False
    )
```
